256 devices in a mesh: img: 8 (over x, core), txt: 32 (over z, y).
Axes of the slice: x: 4, y: 4, z: 8, core: 2. Of those that a mesh axis runs over, the one named last changes fastest.
Arguments:
- picture_embedding_matrix: bfloat16 [8192, 1280], P(('img', 'txt')), may hold values from -0.5 to 0.5
- caption_embedding_matrix: bfloat16 [8192, 1280], P(('txt', 'img')), may hold values from -0.5 to 0.5
- log_scaling_parameter: float32 [1], replicated, may hold values from 2.3 to 5.7
Outputs:
- grad_image: bfloat16 [8192, 1280], P(('img', 'txt'))
- grad_text: bfloat16 [8192, 1280], P(('txt', 'img'))
- loss: float32 [1], replicated
- temp_grad: float32 [1], replicated
The draws below stay inside these ranges and needn't reach their ends.
All inputs are finite; a program needn't handle non-finite values.
Results may differ from the reference program's by a relative error of at most 0.019.
Values may be sent and summed in bfloat16 or wider, within the bound.
No kernel may reach another device: no remote copies, remote signals or barrier semaphores. Data moves between devices by JAX's collectives and lax.ppermute only.
A program may use at most 64 MiB of HBM per device.

```python
import jax
import jax.numpy as jnp
from jax import lax

D = 1280
B = 8192
IMG_BLOCK = 1024
TXT_BLOCK = 256
N_IMG = 8
N_TXT = 32


def shared_normals(key):
    return jax.random.normal(jax.random.fold_in(key, 7), (B, D), jnp.float32)


def position_share(height, power):
    fraction = jnp.arange(B, dtype=jnp.float32) / B
    return (height * (1.0 - fraction) ** power)[:, None]


def draw_picture_embedding_matrix(key, part):
    shared = shared_normals(key)
    unit_scale = D ** (-0.5)
    values = shared * unit_scale
    return jnp.clip(values, -0.5, 0.5).astype(jnp.bfloat16)


def draw_caption_embedding_matrix(key, part):
    shared = shared_normals(key)
    key = jax.random.fold_in(key, 2)
    unit_scale = D ** (-0.5)
    text_noise = jax.random.normal(jax.random.fold_in(key, 4), (B, D), jnp.float32)
    values = (position_share(3.0, 1.0) * shared + text_noise) * unit_scale
    return jnp.clip(values, -0.5, 0.5).astype(jnp.bfloat16)


def draw_log_scaling_parameter(key, part):
    key = jax.random.fold_in(key, 3)
    lower, upper = (2.3, 3.9)
    return jax.random.uniform(key, (1,), jnp.float32, lower, upper)


def setup_inputs(seed: int = 0) -> dict:
    seeds = jax.random.split(jax.random.key(seed), 4)
    return {
        "picture_embedding_matrix": draw_picture_embedding_matrix(jax.random.fold_in(seeds[3], 71), 0),
        "caption_embedding_matrix": draw_caption_embedding_matrix(jax.random.fold_in(seeds[3], 71), 0),
        "log_scaling_parameter": draw_log_scaling_parameter(jax.random.fold_in(seeds[3], 71), 0),
    }


def unit_rows(features):
    values = features.astype(jnp.float32)
    inverse_norm_factor = lax.rsqrt(lax.optimization_barrier(jnp.sum(values * values, axis=1, keepdims=True)) + 1e-06)
    return (values * inverse_norm_factor, inverse_norm_factor)

def unit_sphere_backward(gradient, direction, inverse_norm_factor):
    inner = lax.optimization_barrier(jnp.sum(direction * gradient, axis=1, keepdims=True))
    return ((gradient - direction * inner) * inverse_norm_factor).astype(jnp.bfloat16)

def reference(picture_embedding_matrix, caption_embedding_matrix, log_scaling_parameter):
    fitted_similarity_scaling = jnp.exp(log_scaling_parameter[0])
    img_dir, img_inv = unit_rows(picture_embedding_matrix)
    txt_dir, txt_inv = unit_rows(caption_embedding_matrix)
    img_unit = img_dir.astype(jnp.bfloat16)
    txt_unit = txt_dir.astype(jnp.bfloat16)
    img_blocks = img_unit.reshape(N_IMG, IMG_BLOCK, D)
    txt_blocks = txt_unit.reshape(N_TXT, TXT_BLOCK, D)
    block_starts = jnp.arange(N_IMG, dtype=jnp.int32) * IMG_BLOCK
    columns = jnp.arange(B, dtype=jnp.int32)

    def logits_of(img_piece):
        return fitted_similarity_scaling * jnp.dot(img_piece, txt_unit.T, preferred_element_type=jnp.float32)

    def first_pass(carried, scan_item):
        col_peak, col_total = carried
        img_piece, row_start = scan_item
        logits = logits_of(img_piece)
        entrywise_maximum_along_line = lax.optimization_barrier(jnp.max(logits, axis=1))
        row_lse = entrywise_maximum_along_line + jnp.log(lax.optimization_barrier(jnp.sum(jnp.exp(logits - entrywise_maximum_along_line[:, None]), axis=1)))
        new_peak = jnp.maximum(col_peak, lax.optimization_barrier(jnp.max(logits, axis=0)))
        col_total = col_total * jnp.exp(col_peak - new_peak) + lax.optimization_barrier(jnp.sum(jnp.exp(logits - new_peak[None, :]), axis=0))
        return ((new_peak, col_total), row_lse)
    start_state = (jnp.full((B,), -jnp.inf, jnp.float32), jnp.zeros((B,), jnp.float32))
    (col_peak, col_total), row_lse = lax.scan(first_pass, start_state, (img_blocks, block_starts))
    col_lse = col_peak + jnp.log(col_total)

    def second_pass(carried, scan_item):
        txt_grad, temp_sum, pos_sum = carried
        img_piece, row_start, lse_part = scan_item
        logits = logits_of(img_piece)
        row_index = row_start + jnp.arange(IMG_BLOCK, dtype=jnp.int32)
        matching_pair_mask = row_index[:, None] == columns[None, :]
        weights = jnp.exp(logits - lse_part[:, None]) + jnp.exp(logits - col_lse[None, :]) - 2.0 * matching_pair_mask.astype(jnp.float32)
        logit_grads = (0.5 * weights).astype(jnp.bfloat16)
        derivative_portions = logit_grads.reshape(IMG_BLOCK, N_TXT, TXT_BLOCK).transpose(1, 0, 2)

        def per_text(running, pair):
            grad_piece, txt_piece = pair
            term = (fitted_similarity_scaling * jnp.dot(grad_piece, txt_piece, preferred_element_type=jnp.float32)).astype(jnp.bfloat16)
            return (running + term.astype(jnp.float32), None)
        img_grad, unused = lax.scan(per_text, jnp.zeros((IMG_BLOCK, D), jnp.float32), (derivative_portions, txt_blocks))
        txt_term = (fitted_similarity_scaling * jnp.dot(logit_grads.T, img_piece, preferred_element_type=jnp.float32)).astype(jnp.bfloat16)
        txt_grad = txt_grad + txt_term.astype(jnp.float32)
        temp_sum = temp_sum + jnp.sum(logit_grads.astype(jnp.float32) * logits)
        pos_sum = pos_sum + jnp.sum(jnp.where(matching_pair_mask, logits, jnp.float32(0.0)))
        return ((txt_grad, temp_sum, pos_sum), img_grad)
    start_state = (jnp.zeros((B, D), jnp.float32), jnp.float32(0.0), jnp.float32(0.0))
    (txt_grad, temp_sum, pos_sum), img_grad = lax.scan(second_pass, start_state, (img_blocks, block_starts, row_lse))
    img_grad = img_grad.reshape(B, D)
    loss = (jnp.sum(row_lse) + jnp.sum(col_lse) - 2.0 * pos_sum) / (2 * B)
    temp_grad = temp_sum / B
    return (unit_sphere_backward(img_grad, img_dir, img_inv), unit_sphere_backward(txt_grad, txt_dir, txt_inv), loss.reshape(1), temp_grad.reshape(1))
```

```python
import jax
import jax.numpy as jnp
from jax import lax
from jax.experimental import pallas as pl
from jax.experimental.pallas import tpu as pltpu
from jax.sharding import Mesh, PartitionSpec as P

F32 = jnp.float32
BF16 = jnp.bfloat16
NX, NC, NZ, NY = 4, 2, 8, 4
NXY = NX * NY
OWN = 32
TILE = 512
LANE = 128
NB = TILE // LANE
PAD = 128
VMEM_LIMIT = 48 * 1024 * 1024
PARAMS = pltpu.CompilerParams(vmem_limit_bytes=VMEM_LIMIT)


def inverse_norm(values):
    return lax.rsqrt(jnp.sum(values * values, axis=1, keepdims=True) + 1e-06)


def position():
    return lax.axis_index("x"), lax.axis_index("c"), lax.axis_index("z"), lax.axis_index("y")


def rows_at(start, size):
    return pl.ds(pl.multiple_of(start, size), size)


def normalize_kernel(pic_ref, cap_ref, img_ref, txt_ref):
    pic = pic_ref[...].astype(F32)
    img = (pic * inverse_norm(pic)).astype(BF16)
    for slot in range(NXY):
        img_ref[slot] = img
    cap = cap_ref[...].astype(F32)
    txt_ref[...] = (cap * inverse_norm(cap)).astype(BF16)


def scale_row(log_ref):
    return jnp.exp(jnp.full((1, LANE), log_ref[0], F32))


def pair_mask(j, q, x, c, z, y):
    row = lax.broadcasted_iota(jnp.int32, (LANE, 1), 0) + j * LANE
    col = lax.broadcasted_iota(jnp.int32, (1, LANE), 1) + q * LANE
    slot = row // OWN
    image = (((slot // NY) * NC + c) * (NZ * NY) + z * NY + slot % NY) * OWN + row % OWN
    part = col // OWN
    text = (((part % NZ) * NY + y) * (NX * NC) + x * NC + part // NZ) * OWN + col % OWN
    return image == text


def to_lanes(column):
    return jnp.transpose(jnp.broadcast_to(column, (LANE, LANE)))[0:1, :]


def logits_kernel(log_ref, img_ref, own_ref, other_ref, logit_ref, txt_ref, rowp_ref, colp_ref):
    x, c, z, y = position()
    for k in range(NZ):
        start = lax.rem(z - k + NZ, NZ) * OWN
        txt_ref[rows_at(c * (NZ * OWN) + start, OWN), :] = own_ref[k * OWN : (k + 1) * OWN, :]
        txt_ref[rows_at((1 - c) * (NZ * OWN) + start, OWN), :] = other_ref[k * OWN : (k + 1) * OWN, :]
    img = img_ref[...].reshape(TILE, img_ref.shape[2])
    scale = jnp.tile(scale_row(log_ref), (1, NB))
    logit_ref[...] = scale * lax.dot_general(
        img, txt_ref[...], (((1,), (1,)), ((), ())), preferred_element_type=F32
    )
    pos = jnp.zeros((LANE, LANE), F32)
    for j in range(NB):
        piece = logit_ref[j * LANE : (j + 1) * LANE, :]
        peak = jnp.max(piece, axis=1, keepdims=True)
        shifted = jnp.exp(piece - peak)
        total = jnp.sum(shifted, axis=1, keepdims=True)
        mean = to_lanes(jnp.sum(shifted * piece, axis=1, keepdims=True) / total)
        lse = to_lanes(peak + jnp.log(total))
        for slot in range(NXY):
            rowp_ref[slot, j : j + 1, :] = lse
            rowp_ref[slot, NB + j : NB + j + 1, :] = mean
        for q in range(NB):
            pos += jnp.where(pair_mask(j, q, x, c, z, y), piece[:, q * LANE : (q + 1) * LANE], 0.0)
    for q in range(NB):
        piece = logit_ref[:, q * LANE : (q + 1) * LANE]
        peak = jnp.max(piece, axis=0, keepdims=True)
        shifted = jnp.exp(piece - peak)
        total = jnp.sum(shifted, axis=0, keepdims=True)
        colp_ref[q : q + 1, :] = peak + jnp.log(total)
        colp_ref[NB + q : NB + q + 1, :] = jnp.sum(shifted * piece, axis=0, keepdims=True) / total
    pos = jnp.sum(pos, axis=0, keepdims=True)
    first = lax.broadcasted_iota(jnp.int32, (2 * NB, LANE), 0) == 0
    colp_ref[2 * NB :, :] = jnp.where(first, pos, 0.0)


def combine(lse, mean):
    peak = jnp.max(lse, axis=0)
    weight = jnp.exp(lse - peak)
    total = jnp.sum(weight, axis=0)
    return peak + jnp.log(total), jnp.sum(weight * mean, axis=0) / total


def all_sum(values):
    return jnp.sum(jnp.sum(values, axis=1, keepdims=True), axis=0, keepdims=True)


def scalar_block(source, loss_part, temp_part):
    lane = lax.broadcasted_iota(jnp.int32, (OWN, PAD), 1)
    row = lax.broadcasted_iota(jnp.int32, (OWN, PAD), 0)
    value = jnp.where(lane == source * 8, loss_part, jnp.where(lane == source * 8 + 1, temp_part, 0.0))
    high = value.astype(BF16).astype(F32)
    rest = value - high
    middle = rest.astype(BF16).astype(F32)
    low = rest - middle
    return jnp.where(row == 0, high, jnp.where(row == 1, middle, jnp.where(row == 2, low, 0.0))).astype(BF16)


def grad_kernel(log_ref, logit_ref, img_ref, txt_ref, rowg_ref, *refs):
    colg_refs = refs[:NZ]
    term_ref, keep_ref, send_ref, grad, gradt, colg = refs[NZ:]
    x, c, z, y = position()
    width = txt_ref.shape[1]
    for k in range(NZ):
        start = lax.rem(z - k + NZ, NZ)
        colg[c * NZ + start] = colg_refs[k][0]
        colg[(1 - c) * NZ + start] = colg_refs[k][1]
    row_lse, row_mean = combine(rowg_ref[:, :NB, :], rowg_ref[:, NB:, :])
    col_lse, col_mean = combine(colg[:, :NB, :], colg[:, NB : 2 * NB, :])
    pos = all_sum(jnp.sum(colg[:, 2 * NB :, :], axis=0))
    row_block = scalar_block(z * NC + c, all_sum(row_lse), 0.5 * all_sum(row_mean))
    col_block = scalar_block(x * NY + y, all_sum(col_lse) - 2.0 * pos, 0.5 * all_sum(col_mean) - pos)
    for j in range(NB):
        line = jnp.transpose(jnp.broadcast_to(row_lse[j : j + 1, :], (LANE, LANE)))
        for q in range(NB):
            piece = logit_ref[j * LANE : (j + 1) * LANE, q * LANE : (q + 1) * LANE]
            pair = pair_mask(j, q, x, c, z, y)
            weight = 0.5 * (jnp.exp(piece - line) + jnp.exp(piece - col_lse[q : q + 1, :]))
            weight = weight - jnp.where(pair, 1.0, 0.0)
            grad[j * LANE : (j + 1) * LANE, q * LANE : (q + 1) * LANE] = weight.astype(BF16)
            gradt[q * LANE : (q + 1) * LANE, j * LANE : (j + 1) * LANE] = jnp.transpose(weight).astype(BF16)
    scale = scale_row(log_ref)
    step = 2 * LANE
    scale = jnp.tile(scale, (1, 2))
    half = NZ * OWN
    for start in range(0, width, step):
        span = slice(start, start + step)
        img = img_ref[:, :, span].reshape(TILE, step)
        keep_ref[:, span] = (
            scale * jnp.dot(gradt[rows_at(c * half, half), :], img, preferred_element_type=F32)
        ).astype(BF16)
        send_ref[:, span] = (
            scale * jnp.dot(gradt[rows_at((1 - c) * half, half), :], img, preferred_element_type=F32)
        ).astype(BF16)
        term_ref[:, :, span] = (
            (scale * jnp.dot(grad[...], txt_ref[:, span], preferred_element_type=F32))
            .astype(BF16)
            .reshape(NXY, OWN, step)
        )
    for slot in range(NXY):
        term_ref[slot, :, width:] = col_block
    for k in range(NZ):
        keep_ref[k * OWN : (k + 1) * OWN, width:] = row_block
        send_ref[k * OWN : (k + 1) * OWN, width:] = row_block


def add_kernel(keep_ref, other_ref, *out_refs):
    z = lax.axis_index("z")
    for k in range(NZ):
        rows = rows_at(lax.rem(z + k, NZ) * OWN, OWN)
        out_refs[k][...] = (keep_ref[rows, :].astype(F32) + other_ref[rows, :].astype(F32)).astype(BF16)


def unit_backward(values, gradient):
    inverse = inverse_norm(values)
    direction = values * inverse
    inner = jnp.sum(direction * gradient, axis=1, keepdims=True)
    return ((gradient - direction * inner) * inverse).astype(BF16)


def final_kernel(pic_ref, cap_ref, term_ref, *refs):
    part_refs = refs[:NZ]
    gpic_ref, gcap_ref, loss_ref, temp_ref = refs[NZ:]
    width = pic_ref.shape[1]
    img = term_ref[0].astype(F32)
    for slot in range(1, NXY):
        img += term_ref[slot].astype(F32)
    txt = part_refs[0][...].astype(F32)
    for ref in part_refs[1:]:
        txt += ref[...].astype(F32)
    gpic_ref[...] = unit_backward(pic_ref[...].astype(F32), img[:, :width])
    gcap_ref[...] = unit_backward(cap_ref[...].astype(F32), txt[:, :width])
    scalars = jnp.sum(img[:8, width:], axis=0, keepdims=True) + jnp.sum(txt[:8, width:], axis=0, keepdims=True)
    lane = lax.broadcasted_iota(jnp.int32, (1, PAD), 1) % 8
    pairs = TILE * NXY
    loss_ref[0] = jnp.sum(jnp.where(lane == 0, scalars, 0.0)) / (2 * pairs)
    temp_ref[0] = jnp.sum(jnp.where(lane == 1, scalars, 0.0)) / pairs


def shape(dims, dtype):
    return jax.ShapeDtypeStruct(dims, dtype)


def shift(values, k):
    return lax.ppermute(values, "z", [(i, (i + k) % NZ) for i in range(NZ)])


def swap(values):
    return lax.ppermute(values, "c", [(0, 1), (1, 0)])


def exchange(values):
    return lax.all_to_all(values, ("x", "y"), 0, 0, tiled=True)


VM = pl.BlockSpec(memory_space=pltpu.VMEM)
SM = pl.BlockSpec(memory_space=pltpu.SMEM)


def call(kernel, out_shape, in_specs, out_specs=None, scratch=()):
    return pl.pallas_call(
        kernel,
        out_shape=out_shape,
        in_specs=in_specs,
        out_specs=out_specs if out_specs is not None else [VM] * len(out_shape),
        scratch_shapes=scratch,
        compiler_params=PARAMS,
    )


def shards(pic, cap, log_scale):
    width = pic.shape[1]
    wide = width + PAD
    half = NZ * OWN
    img_out, txt_own = call(
        normalize_kernel,
        [shape((NXY, OWN, width), BF16), shape((OWN, width), BF16)],
        [VM, VM],
    )(pic, cap)
    img = exchange(img_out)
    own = jnp.concatenate([txt_own] + [shift(txt_own, k) for k in range(1, NZ)], axis=0)
    other = swap(own)
    logits, txt, rowp, colp = call(
        logits_kernel,
        [
            shape((TILE, TILE), F32),
            shape((TILE, width), BF16),
            shape((NXY, 2 * NB, LANE), F32),
            shape((4 * NB, LANE), F32),
        ],
        [SM, VM, VM, VM],
    )(log_scale, img, own, other)
    rowg = exchange(rowp)
    colp = jnp.stack([colp, swap(colp)])
    colg = [colp] + [shift(colp, k) for k in range(1, NZ)]
    terms, keep, send = call(
        grad_kernel,
        [shape((NXY, OWN, wide), BF16), shape((half, wide), BF16), shape((half, wide), BF16)],
        [SM] + [VM] * (4 + NZ),
        scratch=[
            pltpu.VMEM((TILE, TILE), BF16),
            pltpu.VMEM((TILE, TILE), BF16),
            pltpu.VMEM((NC * NZ, 4 * NB, LANE), F32),
        ],
    )(log_scale, logits, img, txt, rowg, *colg)
    terms = exchange(terms)
    parts = call(add_kernel, [shape((OWN, wide), BF16)] * NZ, [VM, VM])(keep, swap(send))
    parts = [parts[0]] + [shift(parts[k], k) for k in range(1, NZ)]
    return call(
        final_kernel,
        [shape((OWN, width), BF16), shape((OWN, width), BF16), shape((1,), F32), shape((1,), F32)],
        [VM] * (3 + NZ),
        [VM, VM, SM, SM],
    )(pic, cap, terms, *parts)


def solution(mesh):
    grid = Mesh(mesh.devices.reshape(NX, NC, NZ, NY), ("x", "c", "z", "y"))
    rows = P(("x", "c", "z", "y"), None)
    columns = P(("z", "y", "x", "c"), None)
    return jax.shard_map(
        shards,
        mesh=grid,
        in_specs=(rows, columns, P()),
        out_specs=(rows, columns, P(), P()),
        check_vma=False,
    )
```

```python
import jax
import jax.numpy as jnp
from jax import lax
from jax.experimental import pallas as pl
from jax.experimental.pallas import tpu as pltpu
from jax.sharding import Mesh, PartitionSpec as P

F32 = jnp.float32
BF16 = jnp.bfloat16
NX, NC, NZ, NY = 4, 2, 8, 4
NXY = NX * NY
TURN_X, TURN_Y = 2, 2
FAR = NZ // 2
NEAR = range(1, FAR)
OWN = 32
TILE = 512
LANE = 128
NB = TILE // LANE
PAD = 16
VMEM_LIMIT = 20 * 1024 * 1024
PARAMS = pltpu.CompilerParams(vmem_limit_bytes=VMEM_LIMIT)


def inverse_norm(values):
    return lax.rsqrt(jnp.sum(values * values, axis=1, keepdims=True) + 1e-06)


def position():
    return lax.axis_index("x"), lax.axis_index("c"), lax.axis_index("z"), lax.axis_index("y")


def rows_at(start, size):
    return pl.ds(pl.multiple_of(start, size), size)


def ring(z, steps):
    return lax.rem(z + steps + NZ, NZ)


def arrivals(c, z):
    back = 2 * c - 1
    order = []
    for k in NEAR:
        order += [(c, ring(z, back * k)), (1 - c, ring(z, back * k))]
    return order + [(c, ring(z, FAR))]


def images_kernel(pic_ref, img_ref):
    pic = pic_ref[...].astype(F32)
    img = (pic * inverse_norm(pic)).astype(BF16)
    for slot in range(NXY):
        img_ref[slot] = img


def texts_kernel(cap_ref, other_ref, after_ref, txt_ref):
    for part, ref in enumerate((cap_ref, other_ref)):
        cap = ref[...].astype(F32)
        txt_ref[part] = (cap * inverse_norm(cap)).astype(BF16)


def scale_row(log_ref):
    return jnp.exp(jnp.full((1, LANE), log_ref[0], F32))


def pair_mask(j, q, x, c, z, y):
    row = lax.broadcasted_iota(jnp.int32, (LANE, 1), 0) + j * LANE
    col = lax.broadcasted_iota(jnp.int32, (1, LANE), 1) + q * LANE
    slot = row // OWN
    at_x, at_y = plane_member(slot, c)
    image = ((at_x * NC + c) * (NZ * NY) + z * NY + at_y) * OWN + row % OWN
    part = col // OWN
    text = (((part % NZ) * NY + y) * (NX * NC) + x * NC + part // NZ) * OWN + col % OWN
    return image == text


def similarity(img, txt):
    return lax.dot_general(img, txt, (((1,), (1,)), ((), ())), preferred_element_type=F32)


def to_lanes(column):
    return jnp.transpose(jnp.broadcast_to(column, (LANE, LANE)))[0:1, :]


def logits_kernel(log_ref, img_ref, chip_ref, own_ref, other_ref, txt_ref, rowp_ref, colp_ref, logit_ref):
    x, c, z, y = position()
    for ref, order in (
        (chip_ref, [(c, z), (1 - c, z)]),
        (own_ref, arrivals(c, z)),
        (other_ref, arrivals(1 - c, z)),
    ):
        for k, (core, at) in enumerate(order):
            txt_ref[rows_at((core * NZ + at) * OWN, OWN), :] = ref[k]
    img = img_ref[...].reshape(TILE, img_ref.shape[2])
    scale = jnp.tile(scale_row(log_ref), (1, NB))
    logit_ref[...] = scale * similarity(img, txt_ref[...])
    pos = jnp.zeros((LANE, LANE), F32)
    for j in range(NB):
        piece = logit_ref[j * LANE : (j + 1) * LANE, :]
        peak = jnp.max(piece, axis=1, keepdims=True)
        shifted = jnp.exp(piece - peak)
        total = jnp.sum(shifted, axis=1, keepdims=True)
        mean = to_lanes(jnp.sum(shifted * piece, axis=1, keepdims=True) / total)
        lse = to_lanes(peak + jnp.log(total))
        for slot in range(NXY):
            rowp_ref[slot, j : j + 1, :] = lse
            rowp_ref[slot, NB + j : NB + j + 1, :] = mean
        for q in range(NB):
            pos += jnp.where(pair_mask(j, q, x, c, z, y), piece[:, q * LANE : (q + 1) * LANE], 0.0)
    for q in range(NB):
        piece = logit_ref[:, q * LANE : (q + 1) * LANE]
        peak = jnp.max(piece, axis=0, keepdims=True)
        shifted = jnp.exp(piece - peak)
        total = jnp.sum(shifted, axis=0, keepdims=True)
        colp_ref[q : q + 1, :] = peak + jnp.log(total)
        colp_ref[NB + q : NB + q + 1, :] = jnp.sum(shifted * piece, axis=0, keepdims=True) / total
    pos = jnp.sum(pos, axis=0, keepdims=True)
    first = lax.broadcasted_iota(jnp.int32, (2 * NB, LANE), 0) == 0
    colp_ref[2 * NB :, :] = jnp.where(first, pos, 0.0)


def departures(core, z):
    ahead = 1 - 2 * core
    order = []
    for k in NEAR:
        order += [(core, ring(z, ahead * k)), (1 - core, ring(z, ahead * k))]
    return order + [(core, z), (core, ring(z, FAR))]


def combine(lse, mean):
    peak = jnp.max(lse, axis=0)
    weight = jnp.exp(lse - peak)
    total = jnp.sum(weight, axis=0)
    return peak + jnp.log(total), jnp.sum(weight * mean, axis=0) / total


def all_sum(values):
    return jnp.sum(jnp.sum(values, axis=1, keepdims=True), axis=0, keepdims=True)


def group_at(k):
    return slice(k * OWN, (k + 1) * OWN)


def scalar_block(source, loss_part, temp_part):
    lane = lax.broadcasted_iota(jnp.int32, (PAD, LANE), 1)
    row = lax.broadcasted_iota(jnp.int32, (PAD, LANE), 0)
    value = jnp.where(lane == source * 8, loss_part, jnp.where(lane == source * 8 + 1, temp_part, 0.0))
    high = value.astype(BF16).astype(F32)
    rest = value - high
    middle = rest.astype(BF16).astype(F32)
    low = rest - middle
    return jnp.where(row == 0, high, jnp.where(row == 1, middle, jnp.where(row == 2, low, 0.0))).astype(BF16)


def grad_kernel(
    log_ref, txt_ref, img_ref, rowg_ref, chip_ref, own_ref, other_ref,
    grad_ref, keep_ref, send_ref, columns_ref, logit_ref, gradt, order_gradt, colg,
):
    x, c, z, y = position()
    width = img_ref.shape[2]
    for ref, order in (
        (chip_ref, [(c, z), (1 - c, z)]),
        (own_ref, arrivals(c, z)),
        (other_ref, arrivals(1 - c, z)),
    ):
        for k, (core, at) in enumerate(order):
            colg[core * NZ + at] = ref[k]
    logit_ref[...] = jnp.tile(scale_row(log_ref), (1, NB)) * similarity(
        img_ref[...].reshape(TILE, width), txt_ref[...]
    )
    row_lse, row_mean = combine(rowg_ref[:, :NB, :], rowg_ref[:, NB:, :])
    col_lse, col_mean = combine(colg[:, :NB, :], colg[:, NB : 2 * NB, :])
    pos = all_sum(jnp.sum(colg[:, 2 * NB :, :], axis=0))
    rows_block = scalar_block(z * NC + c, all_sum(row_lse), 0.5 * all_sum(row_mean))
    columns_ref[...] = scalar_block(
        y * NX + x, all_sum(col_lse) - 2.0 * pos, 0.5 * all_sum(col_mean) - pos
    )
    for j in range(NB):
        line = jnp.transpose(jnp.broadcast_to(row_lse[j : j + 1, :], (LANE, LANE)))
        for q in range(NB):
            piece = logit_ref[j * LANE : (j + 1) * LANE, q * LANE : (q + 1) * LANE]
            pair = pair_mask(j, q, x, c, z, y)
            weight = 0.5 * (jnp.exp(piece - line) + jnp.exp(piece - col_lse[q : q + 1, :]))
            weight = weight - jnp.where(pair, 1.0, 0.0)
            grad_ref[j * LANE : (j + 1) * LANE, q * LANE : (q + 1) * LANE] = weight.astype(BF16)
            gradt[q * LANE : (q + 1) * LANE, j * LANE : (j + 1) * LANE] = jnp.transpose(weight).astype(BF16)
    for part, core in enumerate((c, 1 - c)):
        for k, (to, at) in enumerate(departures(core, z)):
            start = (part * NZ + k) * OWN
            order_gradt[start : start + OWN, :] = gradt[rows_at((to * NZ + at) * OWN, OWN), :]
    step = 2 * LANE
    half = NZ * OWN
    scale = jnp.tile(scale_row(log_ref), (1, 2))
    for start in range(0, width, step):
        span = slice(start, start + step)
        img = img_ref[:, :, span].reshape(TILE, step)
        term = (scale * jnp.dot(order_gradt[...], img, preferred_element_type=F32)).astype(BF16)
        for k in range(2):
            group = group_at(start // LANE + k)
            lanes = slice(k * LANE, (k + 1) * LANE)
            keep_ref[:, group, :] = term[:half, lanes].reshape(NZ, OWN, LANE)
            send_ref[:, group, :] = term[half:, lanes].reshape(NZ, OWN, LANE)
    last = width // LANE * OWN
    for k in range(NZ):
        keep_ref[k, last:, :] = rows_block
        send_ref[k, last:, :] = rows_block


def terms_kernel(log_ref, grad_ref, txt_ref, columns_ref, term_ref):
    width = txt_ref.shape[1]
    step = 2 * LANE
    scale = jnp.tile(scale_row(log_ref), (1, 2))
    for start in range(0, width, step):
        term = scale * jnp.dot(grad_ref[...], txt_ref[:, start : start + step], preferred_element_type=F32)
        term = term.astype(BF16)
        for k in range(2):
            lanes = slice(k * LANE, (k + 1) * LANE)
            term_ref[:, group_at(start // LANE + k), :] = term[:, lanes].reshape(NXY, OWN, LANE)
    for slot in range(NXY):
        term_ref[slot, width // LANE * OWN :, :] = columns_ref[...]


def add_kernel(keep_ref, other_ref, term_ref, *out_refs):
    total = (keep_ref[...].astype(F32) + other_ref[...].astype(F32)).astype(BF16)
    one_ref, two_ref, keep_out, far_ref = out_refs[:4]
    one_ref[...] = total[:NC]
    two_ref[...] = total[NC : 3 * NC]
    keep_out[...] = total[3 * NC]
    far_ref[...] = total[3 * NC + 1]


def relay_kernel(one_ref, two_ref, out_ref):
    out_ref[...] = (one_ref[...].astype(F32) + two_ref[NC:].astype(F32)).astype(BF16)


def pass_kernel(one_ref, two_ref, out_ref):
    out_ref[...] = (one_ref[1].astype(F32) + two_ref[1].astype(F32)).astype(BF16)


def unit_backward(values, gradient):
    inverse = inverse_norm(values)
    direction = values * inverse
    inner = jnp.sum(direction * gradient, axis=1, keepdims=True)
    return ((gradient - direction * inner) * inverse).astype(BF16)


def columns_of(values, width):
    return jnp.concatenate([values[group_at(k)] for k in range(width // LANE)], axis=1)


def final_kernel(pic_ref, cap_ref, term_ref, *refs):
    near_refs, part_refs = refs[:2], refs[2:5]
    gpic_ref, gcap_ref, loss_ref, temp_ref = refs[5:]
    width = pic_ref.shape[1]
    img = term_ref[0].astype(F32)
    for slot in range(1, NXY):
        img += term_ref[slot].astype(F32)
    txt = near_refs[0][0].astype(F32)
    for ref in near_refs[1:]:
        txt += ref[0].astype(F32)
    for ref in part_refs:
        txt += ref[...].astype(F32)
    gpic_ref[...] = unit_backward(pic_ref[...].astype(F32), columns_of(img, width))
    gcap_ref[...] = unit_backward(cap_ref[...].astype(F32), columns_of(txt, width))
    last = width // LANE * OWN
    scalars = jnp.sum(img[last : last + 8] + txt[last : last + 8], axis=0, keepdims=True)
    lane = lax.broadcasted_iota(jnp.int32, (1, LANE), 1) % 8
    pairs = TILE * NXY
    loss_ref[0] = jnp.sum(jnp.where(lane == 0, scalars, 0.0)) / (2 * pairs)
    temp_ref[0] = jnp.sum(jnp.where(lane == 1, scalars, 0.0)) / pairs


def shape(dims, dtype):
    return jax.ShapeDtypeStruct(dims, dtype)


def shift(values, k):
    pairs = []
    for core, step in ((0, k), (1, -k)):
        pairs += [(core * NZ + i, core * NZ + (i + step) % NZ) for i in range(NZ)]
    return lax.ppermute(values, ("c", "z"), pairs)


def gather(chip, micros):
    one = shift(chip, 1)
    two = shift(hint(jnp.concatenate([chip, one], axis=0), micros), 2)
    own = jnp.concatenate([one, two, shift(chip[:1], FAR)], axis=0)
    return own, swap(own)


def swap(values):
    return lax.ppermute(values, "c", [(0, 1), (1, 0)])


def plane_member(slot, c):
    return (slot + TURN_X * c) % NX, (slot // NX + TURN_Y * c) % NY


def plane(c, z):
    members = [plane_member(slot, c) for slot in range(NXY)]
    return [((x * NC + c) * NZ + z) * NY + y for x, y in members]


PLANES = [plane(c, z) for c in range(NC) for z in range(NZ)]


def exchange(values):
    return lax.all_to_all(values, ("x", "c", "z", "y"), 0, 0, axis_index_groups=PLANES, tiled=True)


VM = pl.BlockSpec(memory_space=pltpu.VMEM)
ANY = pl.BlockSpec(memory_space=pl.ANY)
SM = pl.BlockSpec(memory_space=pltpu.SMEM)


def call(kernel, out_shape, in_specs, out_specs=None, scratch=(), cost=None, aliases=None):
    return pl.pallas_call(
        kernel,
        name=kernel.__name__,
        out_shape=out_shape,
        in_specs=in_specs,
        out_specs=out_specs if out_specs is not None else [VM] * len(out_shape),
        scratch_shapes=scratch,
        compiler_params=PARAMS,
        cost_estimate=cost,
        input_output_aliases=aliases or {},
    )


def tie_kernel(ref, out_ref):
    pass


def hint(values, micros):
    return call(
        tie_kernel,
        [shape(values.shape, values.dtype)],
        [ANY],
        [ANY],
        aliases={0: 0},
        cost=cost(micros),
    )(values)[0]


def cost(micros):
    return pl.CostEstimate(flops=micros * 1_150_000_000, bytes_accessed=0, transcendentals=0)


def shards(pic, cap, log_scale):
    width = pic.shape[1]
    long = width // LANE * OWN + PAD
    [img_out] = call(images_kernel, [shape((NXY, OWN, width), BF16)], [VM])(pic)
    img = hint(exchange(img_out), 10)
    [chip] = call(texts_kernel, [shape((NC, OWN, width), BF16)], [VM] * 2 + [ANY])(cap, swap(cap), img_out)
    own, other = gather(chip, 10)
    txt, rowp, colp = call(
        logits_kernel,
        [
            shape((TILE, width), BF16),
            shape((NXY, 2 * NB, LANE), F32),
            shape((4 * NB, LANE), F32),
        ],
        [SM, VM, VM, VM, VM],
        scratch=[pltpu.VMEM((TILE, TILE), F32)],
    )(log_scale, img, chip, own, other)
    rowg = hint(exchange(rowp), 30)
    chip = jnp.stack([colp, swap(colp)])
    own, other = gather(chip, 10)
    half = (NZ, long, LANE)
    grad, keep, send, columns = call(
        grad_kernel,
        [
            shape((TILE, TILE), BF16),
            shape(half, BF16),
            shape(half, BF16),
            shape((PAD, LANE), BF16),
        ],
        [SM] + [VM] * 6,
        scratch=[
            pltpu.VMEM((TILE, TILE), F32),
            pltpu.VMEM((TILE, TILE), BF16),
            pltpu.VMEM((TILE, TILE), BF16),
            pltpu.VMEM((NC * NZ, 4 * NB, LANE), F32),
        ],
    )(log_scale, txt, img, rowg, chip, own, other)
    [terms] = call(terms_kernel, [shape((NXY, long, LANE), BF16)], [SM] + [VM] * 3, cost=cost(4))(
        log_scale, grad, txt, columns
    )
    one, two, keep, far, terms = call(
        add_kernel,
        [
            shape((NC, long, LANE), BF16),
            shape((2 * NC, long, LANE), BF16),
            shape((long, LANE), BF16),
            shape((long, LANE), BF16),
            shape((NXY, long, LANE), BF16),
        ],
        [VM, VM, ANY],
        [VM] * 4 + [ANY],
        aliases={2: 4},
    )(keep, swap(send), terms)
    terms = exchange(terms)
    two = shift(two, 2)
    far = shift(far, FAR)
    [one] = call(relay_kernel, [shape((NC, long, LANE), BF16)], [VM] * 2, cost=cost(10))(one, two)
    one = shift(one, 1)
    [passed] = call(pass_kernel, [shape((long, LANE), BF16)], [VM] * 2)(one, two)
    return call(
        final_kernel,
        [shape((OWN, width), BF16), shape((OWN, width), BF16), shape((1,), F32), shape((1,), F32)],
        [VM] * 8,
        [VM, VM, SM, SM],
    )(pic, cap, terms, one, two, keep, far, swap(passed))


def solution(mesh):
    grid = Mesh(mesh.devices.reshape(NX, NC, NZ, NY), ("x", "c", "z", "y"))
    rows = P(("x", "c", "z", "y"), None)
    columns = P(("z", "y", "x", "c"), None)
    return jax.shard_map(
        shards,
        mesh=grid,
        in_specs=(rows, columns, P()),
        out_specs=(rows, columns, P(), P()),
        check_vma=False,
    )
```

```python
import jax
import jax.numpy as jnp
from jax import lax
from jax.experimental import pallas as pl
from jax.experimental.pallas import tpu as pltpu
from jax.sharding import Mesh, PartitionSpec as P

F32 = jnp.float32
BF16 = jnp.bfloat16
NX, NC, NZ, NY = 4, 2, 8, 4
NXY = NX * NY
TURN_X, TURN_Y = 2, 2
FAR = NZ // 2
NEAR = range(1, FAR)
OWN = 32
TILE = 512
LANE = 128
NB = TILE // LANE
PAD = 16
VMEM_LIMIT = 20 * 1024 * 1024
PARAMS = pltpu.CompilerParams(vmem_limit_bytes=VMEM_LIMIT)


def inverse_norm(values):
    return lax.rsqrt(jnp.sum(values * values, axis=1, keepdims=True) + 1e-06)


def position():
    return lax.axis_index("x"), lax.axis_index("c"), lax.axis_index("z"), lax.axis_index("y")


def rows_at(start, size):
    return pl.ds(pl.multiple_of(start, size), size)


def ring(z, steps):
    return lax.rem(z + steps + NZ, NZ)


def arrivals(c, z):
    back = 2 * c - 1
    order = []
    for k in NEAR:
        order += [(c, ring(z, back * k)), (1 - c, ring(z, back * k))]
    return order + [(c, ring(z, FAR))]


def images_kernel(pic_ref, img_ref):
    pic = pic_ref[...].astype(F32)
    img = (pic * inverse_norm(pic)).astype(BF16)
    for slot in range(NXY):
        img_ref[slot] = img


def texts_kernel(cap_ref, other_ref, after_ref, txt_ref):
    for part, ref in enumerate((cap_ref, other_ref)):
        cap = ref[...].astype(F32)
        txt_ref[part] = (cap * inverse_norm(cap)).astype(BF16)


def scale_row(log_ref):
    return jnp.exp(jnp.full((1, LANE), log_ref[0], F32))


def pair_mask(j, q, x, c, z, y):
    row = lax.broadcasted_iota(jnp.int32, (LANE, 1), 0) + j * LANE
    col = lax.broadcasted_iota(jnp.int32, (1, LANE), 1) + q * LANE
    slot = row // OWN
    at_x, at_y = plane_member(slot, c)
    image = ((at_x * NC + c) * (NZ * NY) + z * NY + at_y) * OWN + row % OWN
    part = col // OWN
    text = (((part % NZ) * NY + y) * (NX * NC) + x * NC + part // NZ) * OWN + col % OWN
    return image == text


def similarity(img, txt):
    return lax.dot_general(img, txt, (((1,), (1,)), ((), ())), preferred_element_type=F32)


def to_lanes(column):
    return jnp.transpose(jnp.broadcast_to(column, (LANE, LANE)))[0:1, :]


def ring_blocks(chip_ref, own_ref, other_ref, c, z):
    for ref, order in (
        (chip_ref, [(c, z), (1 - c, z)]),
        (own_ref, arrivals(c, z)),
        (other_ref, arrivals(1 - c, z)),
    ):
        for k, (core, at) in enumerate(order):
            yield ref[k], core * NZ + at


def place_texts(chip_ref, own_ref, other_ref, txt_ref, c, z):
    for block, place in ring_blocks(chip_ref, own_ref, other_ref, c, z):
        txt_ref[rows_at(place * OWN, OWN), :] = block


def logits_kernel(log_ref, img_ref, chip_ref, own_ref, other_ref, rowp_ref, colp_ref, txt_ref, logit_ref):
    x, c, z, y = position()
    place_texts(chip_ref, own_ref, other_ref, txt_ref, c, z)
    img = img_ref[...].reshape(TILE, img_ref.shape[2])
    scale = jnp.tile(scale_row(log_ref), (1, NB))
    logit_ref[...] = scale * similarity(img, txt_ref[...])
    pos = jnp.zeros((LANE, LANE), F32)
    for j in range(NB):
        piece = logit_ref[j * LANE : (j + 1) * LANE, :]
        peak = jnp.max(piece, axis=1, keepdims=True)
        shifted = jnp.exp(piece - peak)
        total = jnp.sum(shifted, axis=1, keepdims=True)
        mean = to_lanes(jnp.sum(shifted * piece, axis=1, keepdims=True) / total)
        lse = to_lanes(peak + jnp.log(total))
        for slot in range(NXY):
            rowp_ref[slot, j : j + 1, :] = lse
            rowp_ref[slot, NB + j : NB + j + 1, :] = mean
        for q in range(NB):
            pos += jnp.where(pair_mask(j, q, x, c, z, y), piece[:, q * LANE : (q + 1) * LANE], 0.0)
    for q in range(NB):
        piece = logit_ref[:, q * LANE : (q + 1) * LANE]
        peak = jnp.max(piece, axis=0, keepdims=True)
        shifted = jnp.exp(piece - peak)
        total = jnp.sum(shifted, axis=0, keepdims=True)
        colp_ref[q : q + 1, :] = peak + jnp.log(total)
        colp_ref[NB + q : NB + q + 1, :] = jnp.sum(shifted * piece, axis=0, keepdims=True) / total
    pos = jnp.sum(pos, axis=0, keepdims=True)
    first = lax.broadcasted_iota(jnp.int32, (2 * NB, LANE), 0) == 0
    colp_ref[2 * NB :, :] = jnp.where(first, pos, 0.0)


def departures(core, z):
    ahead = 1 - 2 * core
    order = []
    for k in NEAR:
        order += [(core, ring(z, ahead * k)), (1 - core, ring(z, ahead * k))]
    return order + [(core, z), (core, ring(z, FAR))]


def combine(lse, mean):
    peak = jnp.max(lse, axis=0)
    weight = jnp.exp(lse - peak)
    total = jnp.sum(weight, axis=0)
    return peak + jnp.log(total), jnp.sum(weight * mean, axis=0) / total


def all_sum(values):
    return jnp.sum(jnp.sum(values, axis=1, keepdims=True), axis=0, keepdims=True)


def group_at(k):
    return slice(k * OWN, (k + 1) * OWN)


def scalar_block(source, loss_part, temp_part):
    lane = lax.broadcasted_iota(jnp.int32, (PAD, LANE), 1)
    row = lax.broadcasted_iota(jnp.int32, (PAD, LANE), 0)
    value = jnp.where(lane == source * 8, loss_part, jnp.where(lane == source * 8 + 1, temp_part, 0.0))
    high = value.astype(BF16).astype(F32)
    rest = value - high
    middle = rest.astype(BF16).astype(F32)
    low = rest - middle
    return jnp.where(row == 0, high, jnp.where(row == 1, middle, jnp.where(row == 2, low, 0.0))).astype(BF16)


def again_kernel(log_ref, img_ref, chip_ref, own_ref, other_ref, row_ref, logit_ref, txt_ref):
    x, c, z, y = position()
    place_texts(chip_ref, own_ref, other_ref, txt_ref, c, z)
    logit_ref[...] = jnp.tile(scale_row(log_ref), (1, NB)) * similarity(
        img_ref[...].reshape(TILE, img_ref.shape[2]), txt_ref[...]
    )


def grad_kernel(
    log_ref, logit_ref, img_ref, row_ref, chip_ref, own_ref, other_ref,
    grad_ref, keep_ref, send_ref, columns_ref, gradt, order_gradt, colg,
):
    x, c, z, y = position()
    width = img_ref.shape[2]
    for block, place in ring_blocks(chip_ref, own_ref, other_ref, c, z):
        colg[place] = block
    row_lse, row_mean = combine(row_ref[:, :NB, :], row_ref[:, NB:, :])
    col_lse, col_mean = combine(colg[:, :NB, :], colg[:, NB : 2 * NB, :])
    pos = all_sum(jnp.sum(colg[:, 2 * NB :, :], axis=0))
    rows_block = scalar_block(z * NC + c, all_sum(row_lse), 0.5 * all_sum(row_mean))
    columns_ref[...] = scalar_block(
        y * NX + x, all_sum(col_lse) - 2.0 * pos, 0.5 * all_sum(col_mean) - pos
    )
    for j in range(NB):
        line = jnp.transpose(jnp.broadcast_to(row_lse[j : j + 1, :], (LANE, LANE)))
        for q in range(NB):
            piece = logit_ref[j * LANE : (j + 1) * LANE, q * LANE : (q + 1) * LANE]
            pair = pair_mask(j, q, x, c, z, y)
            weight = 0.5 * (jnp.exp(piece - line) + jnp.exp(piece - col_lse[q : q + 1, :]))
            weight = weight - jnp.where(pair, 1.0, 0.0)
            grad_ref[j * LANE : (j + 1) * LANE, q * LANE : (q + 1) * LANE] = weight.astype(BF16)
            gradt[q * LANE : (q + 1) * LANE, j * LANE : (j + 1) * LANE] = jnp.transpose(weight).astype(BF16)
    for part, core in enumerate((c, 1 - c)):
        for k, (to, at) in enumerate(departures(core, z)):
            start = (part * NZ + k) * OWN
            order_gradt[start : start + OWN, :] = gradt[rows_at((to * NZ + at) * OWN, OWN), :]
    step = 2 * LANE
    half = NZ * OWN
    scale = jnp.tile(scale_row(log_ref), (1, 2))
    for start in range(0, width, step):
        span = slice(start, start + step)
        img = img_ref[:, :, span].reshape(TILE, step)
        term = (scale * jnp.dot(order_gradt[...], img, preferred_element_type=F32)).astype(BF16)
        for k in range(2):
            group = group_at(start // LANE + k)
            lanes = slice(k * LANE, (k + 1) * LANE)
            keep_ref[:, group, :] = term[:half, lanes].reshape(NZ, OWN, LANE)
            send_ref[:, group, :] = term[half:, lanes].reshape(NZ, OWN, LANE)
    last = width // LANE * OWN
    for k in range(NZ):
        keep_ref[k, last:, :] = rows_block
        send_ref[k, last:, :] = rows_block


def terms_kernel(log_ref, grad_ref, txt_ref, columns_ref, term_ref):
    width = txt_ref.shape[1]
    step = 2 * LANE
    scale = jnp.tile(scale_row(log_ref), (1, 2))
    for start in range(0, width, step):
        term = scale * jnp.dot(grad_ref[...], txt_ref[:, start : start + step], preferred_element_type=F32)
        term = term.astype(BF16)
        for k in range(2):
            lanes = slice(k * LANE, (k + 1) * LANE)
            term_ref[:, group_at(start // LANE + k), :] = term[:, lanes].reshape(NXY, OWN, LANE)
    for slot in range(NXY):
        term_ref[slot, width // LANE * OWN :, :] = columns_ref[...]


def add_kernel(keep_ref, other_ref, term_ref, *out_refs):
    total = (keep_ref[...].astype(F32) + other_ref[...].astype(F32)).astype(BF16)
    one_ref, two_ref, keep_out, far_ref = out_refs[:4]
    one_ref[...] = total[:NC]
    two_ref[...] = total[NC : 3 * NC]
    keep_out[...] = total[3 * NC]
    far_ref[...] = total[3 * NC + 1]


def relay_kernel(one_ref, two_ref, out_ref):
    out_ref[...] = (one_ref[...].astype(F32) + two_ref[NC:].astype(F32)).astype(BF16)


def pass_kernel(one_ref, two_ref, out_ref):
    out_ref[...] = (one_ref[1].astype(F32) + two_ref[1].astype(F32)).astype(BF16)


def unit_backward(values, gradient):
    inverse = inverse_norm(values)
    direction = values * inverse
    inner = jnp.sum(direction * gradient, axis=1, keepdims=True)
    return ((gradient - direction * inner) * inverse).astype(BF16)


def columns_of(values, width):
    return jnp.concatenate([values[group_at(k)] for k in range(width // LANE)], axis=1)


def final_kernel(pic_ref, cap_ref, term_ref, *refs):
    near_refs, part_refs = refs[:2], refs[2:5]
    gpic_ref, gcap_ref, loss_ref, temp_ref = refs[5:]
    width = pic_ref.shape[1]
    img = term_ref[0].astype(F32)
    for slot in range(1, NXY):
        img += term_ref[slot].astype(F32)
    txt = near_refs[0][0].astype(F32)
    for ref in near_refs[1:]:
        txt += ref[0].astype(F32)
    for ref in part_refs:
        txt += ref[...].astype(F32)
    gpic_ref[...] = unit_backward(pic_ref[...].astype(F32), columns_of(img, width))
    gcap_ref[...] = unit_backward(cap_ref[...].astype(F32), columns_of(txt, width))
    last = width // LANE * OWN
    scalars = jnp.sum(img[last : last + 8] + txt[last : last + 8], axis=0, keepdims=True)
    lane = lax.broadcasted_iota(jnp.int32, (1, LANE), 1) % 8
    pairs = TILE * NXY
    loss_ref[0] = jnp.sum(jnp.where(lane == 0, scalars, 0.0)) / (2 * pairs)
    temp_ref[0] = jnp.sum(jnp.where(lane == 1, scalars, 0.0)) / pairs


def shape(dims, dtype):
    return jax.ShapeDtypeStruct(dims, dtype)


def shift(values, k):
    pairs = []
    for core, step in ((0, k), (1, -k)):
        pairs += [(core * NZ + i, core * NZ + (i + step) % NZ) for i in range(NZ)]
    return lax.ppermute(values, ("c", "z"), pairs)


def gather(chip, micros):
    one = shift(chip, 1)
    two = shift(hint(jnp.concatenate([chip, one], axis=0), micros), 2)
    own = jnp.concatenate([one, two, shift(chip[:1], FAR)], axis=0)
    return own, swap(own)


def swap(values):
    return lax.ppermute(values, "c", [(0, 1), (1, 0)])


def plane_member(slot, c):
    return (slot * (1 - c) + (slot // NY + 2) * c) % NX, (slot // NX * (1 - c) + (slot + 2) * c) % NY


def plane(c, z):
    members = [plane_member(slot, c) for slot in range(NXY)]
    return [((x * NC + c) * NZ + z) * NY + y for x, y in members]


PLANES = [plane(c, z) for c in range(NC) for z in range(NZ)]


def exchange(values):
    return lax.all_to_all(values, ("x", "c", "z", "y"), 0, 0, axis_index_groups=PLANES, tiled=True)


VM = pl.BlockSpec(memory_space=pltpu.VMEM)
ANY = pl.BlockSpec(memory_space=pl.ANY)
SM = pl.BlockSpec(memory_space=pltpu.SMEM)


def call(kernel, out_shape, in_specs, out_specs=None, scratch=(), cost=None, aliases=None):
    return pl.pallas_call(
        kernel,
        name=kernel.__name__,
        out_shape=out_shape,
        in_specs=in_specs,
        out_specs=out_specs if out_specs is not None else [VM] * len(out_shape),
        scratch_shapes=scratch,
        compiler_params=PARAMS,
        cost_estimate=cost,
        input_output_aliases=aliases or {},
    )


def tie_kernel(ref, out_ref):
    pass


def hint(values, micros):
    return call(
        tie_kernel,
        [shape(values.shape, values.dtype)],
        [ANY],
        [ANY],
        aliases={0: 0},
        cost=cost(micros),
    )(values)[0]


def cost(micros):
    return pl.CostEstimate(flops=micros * 1_150_000_000, bytes_accessed=0, transcendentals=0)


def shards(pic, cap, log_scale):
    width = pic.shape[1]
    long = width // LANE * OWN + PAD
    [img_out] = call(images_kernel, [shape((NXY, OWN, width), BF16)], [VM])(pic)
    img = hint(exchange(img_out), 10)
    [chip] = call(texts_kernel, [shape((NC, OWN, width), BF16)], [VM] * 2 + [ANY])(cap, swap(cap), img_out)
    own, other = gather(chip, 10)
    rowp, colp = call(
        logits_kernel,
        [
            shape((NXY, 2 * NB, LANE), F32),
            shape((4 * NB, LANE), F32),
        ],
        [SM, VM, VM, VM, VM],
        scratch=[pltpu.VMEM((TILE, width), BF16), pltpu.VMEM((TILE, TILE), F32)],
    )(log_scale, img, chip, own, other)
    rows = exchange(rowp)
    near = jnp.stack([colp, swap(colp)])
    columns = gather(near, 10)
    logits, txt = call(
        again_kernel,
        [shape((TILE, TILE), F32), shape((TILE, width), BF16)],
        [SM] + [VM] * 4 + [ANY],
        cost=cost(30),
    )(log_scale, img, chip, own, other, rows)
    half = (NZ, long, LANE)
    grad, keep, send, scalars = call(
        grad_kernel,
        [
            shape((TILE, TILE), BF16),
            shape(half, BF16),
            shape(half, BF16),
            shape((PAD, LANE), BF16),
        ],
        [SM] + [VM] * 6,
        scratch=[
            pltpu.VMEM((TILE, TILE), BF16),
            pltpu.VMEM((TILE, TILE), BF16),
            pltpu.VMEM((NC * NZ, 4 * NB, LANE), F32),
        ],
    )(log_scale, logits, img, rows, near, *columns)
    [terms] = call(terms_kernel, [shape((NXY, long, LANE), BF16)], [SM] + [VM] * 3, cost=cost(4))(
        log_scale, grad, txt, scalars
    )
    one, two, keep, far, terms = call(
        add_kernel,
        [
            shape((NC, long, LANE), BF16),
            shape((2 * NC, long, LANE), BF16),
            shape((long, LANE), BF16),
            shape((long, LANE), BF16),
            shape((NXY, long, LANE), BF16),
        ],
        [VM, VM, ANY],
        [VM] * 4 + [ANY],
        aliases={2: 4},
    )(keep, swap(send), terms)
    terms = exchange(terms)
    two = shift(two, 2)
    far = shift(far, FAR)
    [one] = call(relay_kernel, [shape((NC, long, LANE), BF16)], [VM] * 2, cost=cost(10))(one, two)
    one = shift(one, 1)
    [passed] = call(pass_kernel, [shape((long, LANE), BF16)], [VM] * 2)(one, two)
    return call(
        final_kernel,
        [shape((OWN, width), BF16), shape((OWN, width), BF16), shape((1,), F32), shape((1,), F32)],
        [VM] * 8,
        [VM, VM, SM, SM],
    )(pic, cap, terms, one, two, keep, far, swap(passed))


def solution(mesh):
    grid = Mesh(mesh.devices.reshape(NX, NC, NZ, NY), ("x", "c", "z", "y"))
    rows = P(("x", "c", "z", "y"), None)
    columns = P(("z", "y", "x", "c"), None)
    return jax.shard_map(
        shards,
        mesh=grid,
        in_specs=(rows, columns, P()),
        out_specs=(rows, columns, P(), P()),
        check_vma=False,
    )
```

```python
import jax
import jax.numpy as jnp
from jax import lax
from jax.experimental import pallas as pl
from jax.experimental.pallas import tpu as pltpu
from jax.sharding import Mesh, PartitionSpec as P

F32 = jnp.float32
BF16 = jnp.bfloat16
NX, NC, NZ, NY = 4, 2, 8, 4
NXY = NX * NY
TURN_X, TURN_Y = 2, 2
FAR = NZ // 2
NEAR = range(1, FAR)
OWN = 32
TILE = 512
LANE = 128
NB = TILE // LANE
PAD = 16
VMEM_LIMIT = 20 * 1024 * 1024
PARAMS = pltpu.CompilerParams(vmem_limit_bytes=VMEM_LIMIT)


def inverse_norm(values):
    return lax.rsqrt(jnp.sum(values * values, axis=1, keepdims=True) + 1e-06)


def position():
    return lax.axis_index("x"), lax.axis_index("c"), lax.axis_index("z"), lax.axis_index("y")


def rows_at(start, size):
    return pl.ds(pl.multiple_of(start, size), size)


def ring(z, steps):
    return lax.rem(z + steps + NZ, NZ)


def arrivals(c, z):
    back = 2 * c - 1
    order = []
    for k in NEAR:
        order += [(c, ring(z, back * k)), (1 - c, ring(z, back * k))]
    return order + [(c, ring(z, FAR))]


def images_kernel(pic_ref, img_ref):
    pic = pic_ref[...].astype(F32)
    img = (pic * inverse_norm(pic)).astype(BF16)
    for slot in range(NXY):
        img_ref[slot] = img


def texts_kernel(cap_ref, other_ref, after_ref, txt_ref):
    for part, ref in enumerate((cap_ref, other_ref)):
        cap = ref[...].astype(F32)
        txt_ref[part] = (cap * inverse_norm(cap)).astype(BF16)


def scale_row(log_ref):
    return jnp.exp(jnp.full((1, LANE), log_ref[0], F32))


def pair_mask(j, q, x, c, z, y, turned=False):
    row = lax.broadcasted_iota(jnp.int32, (LANE, 1), 0) + j * LANE
    col = lax.broadcasted_iota(jnp.int32, (1, LANE), 1) + q * LANE
    image_at, text_at = (col, row) if turned else (row, col)
    slot = image_at // OWN
    at_x, at_y = plane_member(slot, c)
    image = ((at_x * NC + c) * (NZ * NY) + z * NY + at_y) * OWN + image_at % OWN
    part = text_at // OWN
    text = (((part % NZ) * NY + y) * (NX * NC) + x * NC + part // NZ) * OWN + text_at % OWN
    return image == text


def similarity(img, txt):
    return lax.dot_general(img, txt, (((1,), (1,)), ((), ())), preferred_element_type=F32)


def to_lanes(column):
    return jnp.transpose(jnp.broadcast_to(column, (LANE, LANE)))[0:1, :]


def ring_blocks(chip_ref, own_ref, other_ref, c, z):
    for ref, order in (
        (chip_ref, [(c, z), (1 - c, z)]),
        (own_ref, arrivals(c, z)),
        (other_ref, arrivals(1 - c, z)),
    ):
        for k, (core, at) in enumerate(order):
            yield ref[k], core * NZ + at


def place_texts(chip_ref, own_ref, other_ref, txt_ref, c, z):
    for block, place in ring_blocks(chip_ref, own_ref, other_ref, c, z):
        txt_ref[rows_at(place * OWN, OWN), :] = block


def early_kernel(log_ref, img_ref, chip_ref, own_ref, part_ref, txt_ref):
    width = img_ref.shape[2]
    here = NC * OWN
    txt_ref[:here, :] = chip_ref[...].reshape(here, width)
    txt_ref[here:, :] = own_ref[...].reshape(own_ref.shape[0] * OWN, width)
    scale = jnp.tile(scale_row(log_ref), (1, NB))
    part_ref[...] = scale * similarity(txt_ref[...], img_ref[...].reshape(TILE, width))


def logits_kernel(log_ref, img_ref, part_ref, other_ref, rowp_ref, colp_ref, logit_ref):
    x, c, z, y = position()
    width = img_ref.shape[2]
    places = [core * NZ + at for core, at in [(c, z), (1 - c, z), *arrivals(c, z), *arrivals(1 - c, z)]]
    here = part_ref.shape[0]
    scale = jnp.tile(scale_row(log_ref), (1, NB))
    rest = scale * similarity(other_ref[...].reshape(TILE - here, width), img_ref[...].reshape(TILE, width))
    for k, place in enumerate(places):
        start = k * OWN
        block = part_ref[start : start + OWN, :] if start < here else rest[start - here : start - here + OWN, :]
        logit_ref[rows_at(place * OWN, OWN), :] = block
    pos = jnp.zeros((LANE, LANE), F32)
    for j in range(NB):
        piece = logit_ref[j * LANE : (j + 1) * LANE, :]
        peak = jnp.max(piece, axis=1, keepdims=True)
        shifted = jnp.exp(piece - peak)
        total = jnp.sum(shifted, axis=1, keepdims=True)
        colp_ref[j : j + 1, :] = to_lanes(peak + jnp.log(total))
        colp_ref[NB + j : NB + j + 1, :] = to_lanes(jnp.sum(shifted * piece, axis=1, keepdims=True) / total)
        for q in range(NB):
            pair = pair_mask(j, q, x, c, z, y, turned=True)
            pos += jnp.where(pair, piece[:, q * LANE : (q + 1) * LANE], 0.0)
    for q in range(NB):
        piece = logit_ref[:, q * LANE : (q + 1) * LANE]
        peak = jnp.max(piece, axis=0, keepdims=True)
        shifted = jnp.exp(piece - peak)
        total = jnp.sum(shifted, axis=0, keepdims=True)
        lse = peak + jnp.log(total)
        mean = jnp.sum(shifted * piece, axis=0, keepdims=True) / total
        for slot in range(NXY):
            rowp_ref[slot, q : q + 1, :] = lse
            rowp_ref[slot, NB + q : NB + q + 1, :] = mean
    pos = jnp.sum(pos, axis=0, keepdims=True)
    first = lax.broadcasted_iota(jnp.int32, (2 * NB, LANE), 0) == 0
    colp_ref[2 * NB :, :] = jnp.where(first, pos, 0.0)


def departures(core, z):
    ahead = 1 - 2 * core
    order = []
    for k in NEAR:
        order += [(core, ring(z, ahead * k)), (1 - core, ring(z, ahead * k))]
    return order + [(core, z), (core, ring(z, FAR))]


def combine(lse, mean):
    peak = jnp.max(lse, axis=0)
    weight = jnp.exp(lse - peak)
    total = jnp.sum(weight, axis=0)
    return peak + jnp.log(total), jnp.sum(weight * mean, axis=0) / total


def all_sum(values):
    return jnp.sum(jnp.sum(values, axis=1, keepdims=True), axis=0, keepdims=True)


def group_at(k):
    return slice(k * OWN, (k + 1) * OWN)


def scalar_block(source, loss_part, temp_part):
    lane = lax.broadcasted_iota(jnp.int32, (PAD, LANE), 1)
    row = lax.broadcasted_iota(jnp.int32, (PAD, LANE), 0)
    value = jnp.where(lane == source * 8, loss_part, jnp.where(lane == source * 8 + 1, temp_part, 0.0))
    high = value.astype(BF16).astype(F32)
    rest = value - high
    middle = rest.astype(BF16).astype(F32)
    low = rest - middle
    return jnp.where(row == 0, high, jnp.where(row == 1, middle, jnp.where(row == 2, low, 0.0))).astype(BF16)


def again_kernel(log_ref, img_ref, chip_ref, own_ref, other_ref, row_ref, logit_ref, txt_ref):
    x, c, z, y = position()
    place_texts(chip_ref, own_ref, other_ref, txt_ref, c, z)
    logit_ref[...] = jnp.tile(scale_row(log_ref), (1, NB)) * similarity(
        img_ref[...].reshape(TILE, img_ref.shape[2]), txt_ref[...]
    )


def grad_kernel(
    log_ref, logit_ref, img_ref, row_ref, chip_ref, own_ref, other_ref,
    grad_ref, keep_ref, send_ref, columns_ref, gradt, order_gradt, colg,
):
    x, c, z, y = position()
    width = img_ref.shape[2]
    for block, place in ring_blocks(chip_ref, own_ref, other_ref, c, z):
        colg[place] = block
    row_lse, row_mean = combine(row_ref[:, :NB, :], row_ref[:, NB:, :])
    col_lse, col_mean = combine(colg[:, :NB, :], colg[:, NB : 2 * NB, :])
    pos = all_sum(jnp.sum(colg[:, 2 * NB :, :], axis=0))
    rows_block = scalar_block(z * NC + c, all_sum(row_lse), 0.5 * all_sum(row_mean))
    columns_ref[...] = scalar_block(
        y * NX + x, all_sum(col_lse) - 2.0 * pos, 0.5 * all_sum(col_mean) - pos
    )
    for j in range(NB):
        line = jnp.transpose(jnp.broadcast_to(row_lse[j : j + 1, :], (LANE, LANE)))
        for q in range(NB):
            piece = logit_ref[j * LANE : (j + 1) * LANE, q * LANE : (q + 1) * LANE]
            pair = pair_mask(j, q, x, c, z, y)
            weight = 0.5 * (jnp.exp(piece - line) + jnp.exp(piece - col_lse[q : q + 1, :]))
            weight = weight - jnp.where(pair, 1.0, 0.0)
            grad_ref[j * LANE : (j + 1) * LANE, q * LANE : (q + 1) * LANE] = weight.astype(BF16)
            gradt[q * LANE : (q + 1) * LANE, j * LANE : (j + 1) * LANE] = jnp.transpose(weight).astype(BF16)
    for part, core in enumerate((c, 1 - c)):
        for k, (to, at) in enumerate(departures(core, z)):
            start = (part * NZ + k) * OWN
            order_gradt[start : start + OWN, :] = gradt[rows_at((to * NZ + at) * OWN, OWN), :]
    step = 2 * LANE
    half = NZ * OWN
    scale = jnp.tile(scale_row(log_ref), (1, 2))
    for start in range(0, width, step):
        span = slice(start, start + step)
        img = img_ref[:, :, span].reshape(TILE, step)
        term = (scale * jnp.dot(order_gradt[...], img, preferred_element_type=F32)).astype(BF16)
        for k in range(2):
            group = group_at(start // LANE + k)
            lanes = slice(k * LANE, (k + 1) * LANE)
            keep_ref[:, group, :] = term[:half, lanes].reshape(NZ, OWN, LANE)
            send_ref[:, group, :] = term[half:, lanes].reshape(NZ, OWN, LANE)
    last = width // LANE * OWN
    for k in range(NZ):
        keep_ref[k, last:, :] = rows_block
        send_ref[k, last:, :] = rows_block


def terms_kernel(log_ref, grad_ref, txt_ref, columns_ref, term_out, term_ref, sems):
    width = txt_ref.shape[1]
    step = 2 * LANE
    scale = jnp.tile(scale_row(log_ref), (1, 2))
    for slot in range(NXY):
        term_ref[slot, width // LANE * OWN :, :] = columns_ref[...]
    copies = []
    for start in range(0, width, step):
        term = scale * jnp.dot(grad_ref[...], txt_ref[:, start : start + step], preferred_element_type=F32)
        term = term.astype(BF16)
        for k in range(2):
            lanes = slice(k * LANE, (k + 1) * LANE)
            term_ref[:, group_at(start // LANE + k), :] = term[:, lanes].reshape(NXY, OWN, LANE)
        rows = pl.ds(start // LANE * OWN, 2 * OWN + (PAD if start + step == width else 0))
        copies.append(
            pltpu.make_async_copy(term_ref.at[:, rows, :], term_out.at[:, rows, :], sems.at[start // step])
        )
        copies[-1].start()
    for copy in copies:
        copy.wait()


def add_kernel(keep_ref, other_ref, term_ref, *out_refs):
    total = (keep_ref[...].astype(F32) + other_ref[...].astype(F32)).astype(BF16)
    one_ref, two_ref, keep_out, far_ref = out_refs[:4]
    one_ref[...] = total[:NC]
    two_ref[...] = total[NC : 3 * NC]
    keep_out[...] = total[3 * NC]
    far_ref[...] = total[3 * NC + 1]


def relay_kernel(one_ref, two_ref, out_ref):
    out_ref[...] = (one_ref[...].astype(F32) + two_ref[NC:].astype(F32)).astype(BF16)


def pass_kernel(one_ref, two_ref, out_ref):
    out_ref[...] = (one_ref[1].astype(F32) + two_ref[1].astype(F32)).astype(BF16)


def unit_backward(values, gradient):
    inverse = inverse_norm(values)
    direction = values * inverse
    inner = jnp.sum(direction * gradient, axis=1, keepdims=True)
    return ((gradient - direction * inner) * inverse).astype(BF16)


def columns_of(values, width):
    return jnp.concatenate([values[group_at(k)] for k in range(width // LANE)], axis=1)


def final_kernel(pic_ref, cap_ref, term_ref, *refs):
    near_refs, part_refs = refs[:2], refs[2:5]
    gpic_ref, gcap_ref, loss_ref, temp_ref = refs[5:]
    width = pic_ref.shape[1]
    img = term_ref[0].astype(F32)
    for slot in range(1, NXY):
        img += term_ref[slot].astype(F32)
    txt = near_refs[0][0].astype(F32)
    for ref in near_refs[1:]:
        txt += ref[0].astype(F32)
    for ref in part_refs:
        txt += ref[...].astype(F32)
    gpic_ref[...] = unit_backward(pic_ref[...].astype(F32), columns_of(img, width))
    gcap_ref[...] = unit_backward(cap_ref[...].astype(F32), columns_of(txt, width))
    last = width // LANE * OWN
    scalars = jnp.sum(img[last : last + 8] + txt[last : last + 8], axis=0, keepdims=True)
    lane = lax.broadcasted_iota(jnp.int32, (1, LANE), 1) % 8
    pairs = TILE * NXY
    loss_ref[0] = jnp.sum(jnp.where(lane == 0, scalars, 0.0)) / (2 * pairs)
    temp_ref[0] = jnp.sum(jnp.where(lane == 1, scalars, 0.0)) / pairs


def shape(dims, dtype):
    return jax.ShapeDtypeStruct(dims, dtype)


def shift(values, k):
    pairs = []
    for core, step in ((0, k), (1, -k)):
        pairs += [(core * NZ + i, core * NZ + (i + step) % NZ) for i in range(NZ)]
    return lax.ppermute(values, ("c", "z"), pairs)


def gather(chip, micros):
    one = shift(chip, 1)
    two = shift(hint(jnp.concatenate([chip, one], axis=0), micros), 2)
    own = jnp.concatenate([one, two, shift(chip[:1], FAR)], axis=0)
    return own, swap(own)


def swap(values):
    return lax.ppermute(values, "c", [(0, 1), (1, 0)])


def plane_member(slot, c):
    return (slot * (1 - c) + (slot // NY + 2) * c) % NX, (slot // NX * (1 - c) + (slot + 2) * c) % NY


def plane(c, z):
    members = [plane_member(slot, c) for slot in range(NXY)]
    return [((x * NC + c) * NZ + z) * NY + y for x, y in members]


PLANES = [plane(c, z) for c in range(NC) for z in range(NZ)]


def exchange(values):
    return lax.all_to_all(values, ("x", "c", "z", "y"), 0, 0, axis_index_groups=PLANES, tiled=True)


VM = pl.BlockSpec(memory_space=pltpu.VMEM)
ANY = pl.BlockSpec(memory_space=pl.ANY)
SM = pl.BlockSpec(memory_space=pltpu.SMEM)


def call(kernel, out_shape, in_specs, out_specs=None, scratch=(), cost=None, aliases=None):
    return pl.pallas_call(
        kernel,
        name=kernel.__name__,
        out_shape=out_shape,
        in_specs=in_specs,
        out_specs=out_specs if out_specs is not None else [VM] * len(out_shape),
        scratch_shapes=scratch,
        compiler_params=PARAMS,
        cost_estimate=cost,
        input_output_aliases=aliases or {},
    )


def tie_kernel(ref, out_ref):
    pass


def hint(values, micros):
    return call(
        tie_kernel,
        [shape(values.shape, values.dtype)],
        [ANY],
        [ANY],
        aliases={0: 0},
        cost=cost(micros),
    )(values)[0]


def cost(micros):
    return pl.CostEstimate(flops=micros * 1_150_000_000, bytes_accessed=0, transcendentals=0)


def shards(pic, cap, log_scale):
    width = pic.shape[1]
    long = width // LANE * OWN + PAD
    [img_out] = call(images_kernel, [shape((NXY, OWN, width), BF16)], [VM])(pic)
    img = hint(exchange(img_out), 10)
    [chip] = call(texts_kernel, [shape((NC, OWN, width), BF16)], [VM] * 2 + [ANY])(cap, swap(cap), img_out)
    own, other = gather(chip, 10)
    here = (NC + own.shape[0]) * OWN
    [part] = call(
        early_kernel,
        [shape((here, TILE), F32)],
        [SM] + [VM] * 3,
        scratch=[pltpu.VMEM((here, width), BF16)],
        cost=cost(3),
    )(log_scale, img, chip, own)
    rowp, colp = call(
        logits_kernel,
        [shape((NXY, 2 * NB, LANE), F32), shape((4 * NB, LANE), F32)],
        [SM, VM, VM, VM],
        scratch=[pltpu.VMEM((TILE, TILE), F32)],
    )(log_scale, img, part, other)
    rows = exchange(rowp)
    near = jnp.stack([colp, swap(colp)])
    columns = gather(near, 10)
    logits, txt = call(
        again_kernel,
        [shape((TILE, TILE), F32), shape((TILE, width), BF16)],
        [SM] + [VM] * 4 + [ANY],
        cost=cost(30),
    )(log_scale, img, chip, own, other, rows)
    half = (NZ, long, LANE)
    grad, keep, send, scalars = call(
        grad_kernel,
        [
            shape((TILE, TILE), BF16),
            shape(half, BF16),
            shape(half, BF16),
            shape((PAD, LANE), BF16),
        ],
        [SM] + [VM] * 6,
        scratch=[
            pltpu.VMEM((TILE, TILE), BF16),
            pltpu.VMEM((TILE, TILE), BF16),
            pltpu.VMEM((NC * NZ, 4 * NB, LANE), F32),
        ],
    )(log_scale, logits, img, rows, near, *columns)
    [terms] = call(
        terms_kernel,
        [shape((NXY, long, LANE), BF16)],
        [SM] + [VM] * 3,
        [ANY],
        scratch=[pltpu.VMEM((NXY, long, LANE), BF16), pltpu.SemaphoreType.DMA((width // (2 * LANE),))],
        cost=cost(4),
    )(log_scale, grad, txt, scalars)
    one, two, keep, far, terms = call(
        add_kernel,
        [
            shape((NC, long, LANE), BF16),
            shape((2 * NC, long, LANE), BF16),
            shape((long, LANE), BF16),
            shape((long, LANE), BF16),
            shape((NXY, long, LANE), BF16),
        ],
        [VM, VM, ANY],
        [VM] * 4 + [ANY],
        aliases={2: 4},
    )(keep, swap(send), terms)
    terms = exchange(terms)
    two = shift(two, 2)
    far = shift(far, FAR)
    [one] = call(relay_kernel, [shape((NC, long, LANE), BF16)], [VM] * 2, cost=cost(10))(one, two)
    one = shift(one, 1)
    [passed] = call(pass_kernel, [shape((long, LANE), BF16)], [VM] * 2)(one, two)
    return call(
        final_kernel,
        [shape((OWN, width), BF16), shape((OWN, width), BF16), shape((1,), F32), shape((1,), F32)],
        [VM] * 8,
        [VM, VM, SM, SM],
    )(pic, cap, terms, one, two, keep, far, swap(passed))


def solution(mesh):
    grid = Mesh(mesh.devices.reshape(NX, NC, NZ, NY), ("x", "c", "z", "y"))
    rows = P(("x", "c", "z", "y"), None)
    columns = P(("z", "y", "x", "c"), None)
    return jax.shard_map(
        shards,
        mesh=grid,
        in_specs=(rows, columns, P()),
        out_specs=(rows, columns, P(), P()),
        check_vma=False,
    )
```

```python
import jax
import jax.numpy as jnp
from jax import lax
from jax.experimental import pallas as pl
from jax.experimental.pallas import tpu as pltpu
from jax.sharding import Mesh, PartitionSpec as P

F32 = jnp.float32
BF16 = jnp.bfloat16
NX, NC, NZ, NY = 4, 2, 8, 4
NXY = NX * NY
TURN_X, TURN_Y = 2, 2
FAR = NZ // 2
NEAR = range(1, FAR)
OWN = 32
TILE = 512
LANE = 128
NB = TILE // LANE
PAD = 16
VMEM_LIMIT = 20 * 1024 * 1024
PARAMS = pltpu.CompilerParams(vmem_limit_bytes=VMEM_LIMIT)


def inverse_norm(values):
    return lax.rsqrt(jnp.sum(values * values, axis=1, keepdims=True) + 1e-06)


def position():
    return lax.axis_index("x"), lax.axis_index("c"), lax.axis_index("z"), lax.axis_index("y")


def rows_at(start, size):
    return pl.ds(pl.multiple_of(start, size), size)


def ring(z, steps):
    return lax.rem(z + steps + NZ, NZ)


def arrivals(c, z):
    back = 2 * c - 1
    order = []
    for k in NEAR:
        order += [(c, ring(z, back * k)), (1 - c, ring(z, back * k))]
    return order + [(c, ring(z, FAR))]


def images_kernel(pic_ref, img_ref):
    pic = pic_ref[...].astype(F32)
    img = (pic * inverse_norm(pic)).astype(BF16)
    for slot in range(NXY):
        img_ref[slot] = img


def texts_kernel(cap_ref, other_ref, after_ref, txt_ref):
    for part, ref in enumerate((cap_ref, other_ref)):
        cap = ref[...].astype(F32)
        txt_ref[part] = (cap * inverse_norm(cap)).astype(BF16)


def scale_row(log_ref):
    return jnp.exp(jnp.full((1, LANE), log_ref[0], F32))


def pair_mask(j, q, x, c, z, y, turned=False):
    row = lax.broadcasted_iota(jnp.int32, (LANE, 1), 0) + j * LANE
    col = lax.broadcasted_iota(jnp.int32, (1, LANE), 1) + q * LANE
    image_at, text_at = (col, row) if turned else (row, col)
    slot = image_at // OWN
    at_x, at_y = plane_member(slot, c)
    image = ((at_x * NC + c) * (NZ * NY) + z * NY + at_y) * OWN + image_at % OWN
    part = text_at // OWN
    text = (((part % NZ) * NY + y) * (NX * NC) + x * NC + part // NZ) * OWN + text_at % OWN
    return image == text


def similarity(img, txt):
    return lax.dot_general(img, txt, (((1,), (1,)), ((), ())), preferred_element_type=F32)


def to_lanes(column):
    return jnp.transpose(jnp.broadcast_to(column, (LANE, LANE)))[0:1, :]


def ring_blocks(chip_ref, own_ref, other_ref, c, z):
    for ref, order in (
        (chip_ref, [(c, z), (1 - c, z)]),
        (own_ref, arrivals(c, z)),
        (other_ref, arrivals(1 - c, z)),
    ):
        for k, (core, at) in enumerate(order):
            yield ref[k], core * NZ + at


def place_texts(chip_ref, own_ref, other_ref, txt_ref, c, z):
    for block, place in ring_blocks(chip_ref, own_ref, other_ref, c, z):
        txt_ref[rows_at(place * OWN, OWN), :] = block


def early_kernel(log_ref, img_ref, chip_ref, own_ref, part_ref, txt_ref):
    width = img_ref.shape[2]
    here = NC * OWN
    txt_ref[:here, :] = chip_ref[...].reshape(here, width)
    txt_ref[here:, :] = own_ref[...].reshape(own_ref.shape[0] * OWN, width)
    scale = jnp.tile(scale_row(log_ref), (1, NB))
    part_ref[...] = scale * similarity(txt_ref[...], img_ref[...].reshape(TILE, width))


def logits_kernel(log_ref, img_ref, part_ref, other_ref, rowp_ref, colp_ref, logit_ref):
    x, c, z, y = position()
    width = img_ref.shape[2]
    places = [core * NZ + at for core, at in [(c, z), (1 - c, z), *arrivals(c, z), *arrivals(1 - c, z)]]
    here = part_ref.shape[0]
    scale = jnp.tile(scale_row(log_ref), (1, NB))
    rest = scale * similarity(other_ref[...].reshape(TILE - here, width), img_ref[...].reshape(TILE, width))
    for k, place in enumerate(places):
        start = k * OWN
        block = part_ref[start : start + OWN, :] if start < here else rest[start - here : start - here + OWN, :]
        logit_ref[rows_at(place * OWN, OWN), :] = block
    pos = jnp.zeros((LANE, LANE), F32)
    for j in range(NB):
        piece = logit_ref[j * LANE : (j + 1) * LANE, :]
        peak = jnp.max(piece, axis=1, keepdims=True)
        shifted = jnp.exp(piece - peak)
        total = jnp.sum(shifted, axis=1, keepdims=True)
        colp_ref[j : j + 1, :] = to_lanes(peak + jnp.log(total))
        colp_ref[NB + j : NB + j + 1, :] = to_lanes(jnp.sum(shifted * piece, axis=1, keepdims=True) / total)
        for q in range(NB):
            pair = pair_mask(j, q, x, c, z, y, turned=True)
            pos += jnp.where(pair, piece[:, q * LANE : (q + 1) * LANE], 0.0)
    for q in range(NB):
        piece = logit_ref[:, q * LANE : (q + 1) * LANE]
        peak = jnp.max(piece, axis=0, keepdims=True)
        shifted = jnp.exp(piece - peak)
        total = jnp.sum(shifted, axis=0, keepdims=True)
        lse = peak + jnp.log(total)
        mean = jnp.sum(shifted * piece, axis=0, keepdims=True) / total
        for slot in range(NXY):
            rowp_ref[slot, q : q + 1, :] = lse
            rowp_ref[slot, NB + q : NB + q + 1, :] = mean
    pos = jnp.sum(pos, axis=0, keepdims=True)
    first = lax.broadcasted_iota(jnp.int32, (2 * NB, LANE), 0) == 0
    colp_ref[2 * NB :, :] = jnp.where(first, pos, 0.0)


def departures(core, z):
    ahead = 1 - 2 * core
    order = []
    for k in NEAR:
        order += [(core, ring(z, ahead * k)), (1 - core, ring(z, ahead * k))]
    return order + [(core, z), (core, ring(z, FAR))]


def combine(lse, mean):
    peak = jnp.max(lse, axis=0)
    weight = jnp.exp(lse - peak)
    total = jnp.sum(weight, axis=0)
    return peak + jnp.log(total), jnp.sum(weight * mean, axis=0) / total


def all_sum(values):
    return jnp.sum(jnp.sum(values, axis=1, keepdims=True), axis=0, keepdims=True)


def group_at(k):
    return slice(k * OWN, (k + 1) * OWN)


def scalar_block(source, loss_part, temp_part):
    lane = lax.broadcasted_iota(jnp.int32, (PAD, LANE), 1)
    row = lax.broadcasted_iota(jnp.int32, (PAD, LANE), 0)
    value = jnp.where(lane == source * 8, loss_part, jnp.where(lane == source * 8 + 1, temp_part, 0.0))
    high = value.astype(BF16).astype(F32)
    rest = value - high
    middle = rest.astype(BF16).astype(F32)
    low = rest - middle
    return jnp.where(row == 0, high, jnp.where(row == 1, middle, jnp.where(row == 2, low, 0.0))).astype(BF16)


def again_kernel(log_ref, img_ref, chip_ref, own_ref, other_ref, row_ref, logit_ref, txt_ref):
    x, c, z, y = position()
    place_texts(chip_ref, own_ref, other_ref, txt_ref, c, z)
    logit_ref[...] = jnp.tile(scale_row(log_ref), (1, NB)) * similarity(
        img_ref[...].reshape(TILE, img_ref.shape[2]), txt_ref[...]
    )


def grad_kernel(
    log_ref, logit_ref, img_ref, row_ref, chip_ref, own_ref, other_ref,
    grad_ref, keep_ref, send_ref, columns_ref, gradt, order_gradt, colg,
):
    x, c, z, y = position()
    width = img_ref.shape[2]
    for block, place in ring_blocks(chip_ref, own_ref, other_ref, c, z):
        colg[place] = block
    row_lse, row_mean = combine(row_ref[:, :NB, :], row_ref[:, NB:, :])
    col_lse, col_mean = combine(colg[:, :NB, :], colg[:, NB : 2 * NB, :])
    pos = all_sum(jnp.sum(colg[:, 2 * NB :, :], axis=0))
    rows_block = scalar_block(z * NC + c, all_sum(row_lse), 0.5 * all_sum(row_mean))
    columns_ref[...] = scalar_block(
        y * NX + x, all_sum(col_lse) - 2.0 * pos, 0.5 * all_sum(col_mean) - pos
    )
    for j in range(NB):
        line = jnp.transpose(jnp.broadcast_to(row_lse[j : j + 1, :], (LANE, LANE)))
        for q in range(NB):
            piece = logit_ref[j * LANE : (j + 1) * LANE, q * LANE : (q + 1) * LANE]
            pair = pair_mask(j, q, x, c, z, y)
            weight = 0.5 * (jnp.exp(piece - line) + jnp.exp(piece - col_lse[q : q + 1, :]))
            weight = weight - jnp.where(pair, 1.0, 0.0)
            grad_ref[j * LANE : (j + 1) * LANE, q * LANE : (q + 1) * LANE] = weight.astype(BF16)
            gradt[q * LANE : (q + 1) * LANE, j * LANE : (j + 1) * LANE] = jnp.transpose(weight).astype(BF16)
    for part, core in enumerate((c, 1 - c)):
        for k, (to, at) in enumerate(departures(core, z)):
            start = (part * NZ + k) * OWN
            order_gradt[start : start + OWN, :] = gradt[rows_at((to * NZ + at) * OWN, OWN), :]
    step = 2 * LANE
    half = NZ * OWN
    scale = jnp.tile(scale_row(log_ref), (1, 2))
    for start in range(0, width, step):
        span = slice(start, start + step)
        img = img_ref[:, :, span].reshape(TILE, step)
        term = (scale * jnp.dot(order_gradt[...], img, preferred_element_type=F32)).astype(BF16)
        for k in range(2):
            group = group_at(start // LANE + k)
            lanes = slice(k * LANE, (k + 1) * LANE)
            keep_ref[:, group, :] = term[:half, lanes].reshape(NZ, OWN, LANE)
            send_ref[:, group, :] = term[half:, lanes].reshape(NZ, OWN, LANE)
    last = width // LANE * OWN
    for k in range(NZ):
        keep_ref[k, last:, :] = rows_block
        send_ref[k, last:, :] = rows_block


def terms_kernel(log_ref, grad_ref, txt_ref, columns_ref, term_out, term_ref, sems):
    width = txt_ref.shape[1]
    step = 2 * LANE
    scale = jnp.tile(scale_row(log_ref), (1, 2))
    for slot in range(NXY):
        term_ref[slot, width // LANE * OWN :, :] = columns_ref[...]
    copies = []
    for start in range(0, width, step):
        term = scale * jnp.dot(grad_ref[...], txt_ref[:, start : start + step], preferred_element_type=F32)
        term = term.astype(BF16)
        for k in range(2):
            lanes = slice(k * LANE, (k + 1) * LANE)
            term_ref[:, group_at(start // LANE + k), :] = term[:, lanes].reshape(NXY, OWN, LANE)
        rows = pl.ds(start // LANE * OWN, 2 * OWN + (PAD if start + step == width else 0))
        copies.append(
            pltpu.make_async_copy(term_ref.at[:, rows, :], term_out.at[:, rows, :], sems.at[start // step])
        )
        copies[-1].start()
    for copy in copies:
        copy.wait()


def add_kernel(keep_ref, other_ref, term_ref, *out_refs):
    total = (keep_ref[...].astype(F32) + other_ref[...].astype(F32)).astype(BF16)
    one_ref, two_ref, keep_out, far_ref = out_refs[:4]
    one_ref[...] = total[:NC]
    two_ref[...] = total[NC : 3 * NC]
    keep_out[...] = total[3 * NC]
    far_ref[...] = total[3 * NC + 1]


def relay_kernel(one_ref, two_ref, out_ref):
    out_ref[...] = (one_ref[...].astype(F32) + two_ref[NC:].astype(F32)).astype(BF16)


def pass_kernel(one_ref, two_ref, far_ref, out_ref):
    out_ref[...] = (one_ref[1].astype(F32) + two_ref[1].astype(F32)).astype(BF16)


def unit_backward(values, gradient):
    inverse = inverse_norm(values)
    direction = values * inverse
    inner = jnp.sum(direction * gradient, axis=1, keepdims=True)
    return ((gradient - direction * inner) * inverse).astype(BF16)


def columns_of(values, width):
    return jnp.concatenate([values[group_at(k)] for k in range(width // LANE)], axis=1)


def final_kernel(pic_ref, cap_ref, term_ref, *refs):
    near_refs, part_refs = refs[:2], refs[2:5]
    gpic_ref, gcap_ref, loss_ref, temp_ref = refs[5:]
    width = pic_ref.shape[1]
    img = term_ref[0].astype(F32)
    for slot in range(1, NXY):
        img += term_ref[slot].astype(F32)
    txt = near_refs[0][0].astype(F32)
    for ref in near_refs[1:]:
        txt += ref[0].astype(F32)
    for ref in part_refs:
        txt += ref[...].astype(F32)
    gpic_ref[...] = unit_backward(pic_ref[...].astype(F32), columns_of(img, width))
    gcap_ref[...] = unit_backward(cap_ref[...].astype(F32), columns_of(txt, width))
    last = width // LANE * OWN
    scalars = jnp.sum(img[last : last + 8] + txt[last : last + 8], axis=0, keepdims=True)
    lane = lax.broadcasted_iota(jnp.int32, (1, LANE), 1) % 8
    pairs = TILE * NXY
    loss_ref[0] = jnp.sum(jnp.where(lane == 0, scalars, 0.0)) / (2 * pairs)
    temp_ref[0] = jnp.sum(jnp.where(lane == 1, scalars, 0.0)) / pairs


def shape(dims, dtype):
    return jax.ShapeDtypeStruct(dims, dtype)


def shift(values, k):
    pairs = []
    for core, step in ((0, k), (1, -k)):
        pairs += [(core * NZ + i, core * NZ + (i + step) % NZ) for i in range(NZ)]
    return lax.ppermute(values, ("c", "z"), pairs)


def gather(chip, micros):
    one = shift(chip, 1)
    two = shift(hint(jnp.concatenate([chip, one], axis=0), micros), 2)
    own = jnp.concatenate([one, two, shift(chip[:1], FAR)], axis=0)
    return own, swap(own)


def swap(values):
    return lax.ppermute(values, "c", [(0, 1), (1, 0)])


def plane_member(slot, c):
    return (slot * (1 - c) + (slot // NY + 2) * c) % NX, (slot // NX * (1 - c) + (slot + 2) * c) % NY


def plane(c, z):
    members = [plane_member(slot, c) for slot in range(NXY)]
    return [((x * NC + c) * NZ + z) * NY + y for x, y in members]


PLANES = [plane(c, z) for c in range(NC) for z in range(NZ)]


def exchange(values):
    return lax.all_to_all(values, ("x", "c", "z", "y"), 0, 0, axis_index_groups=PLANES, tiled=True)


VM = pl.BlockSpec(memory_space=pltpu.VMEM)
ANY = pl.BlockSpec(memory_space=pl.ANY)
SM = pl.BlockSpec(memory_space=pltpu.SMEM)


def call(kernel, out_shape, in_specs, out_specs=None, scratch=(), cost=None, aliases=None):
    return pl.pallas_call(
        kernel,
        name=kernel.__name__,
        out_shape=out_shape,
        in_specs=in_specs,
        out_specs=out_specs if out_specs is not None else [VM] * len(out_shape),
        scratch_shapes=scratch,
        compiler_params=PARAMS,
        cost_estimate=cost,
        input_output_aliases=aliases or {},
    )


def tie_kernel(ref, out_ref):
    pass


def hint(values, micros):
    return call(
        tie_kernel,
        [shape(values.shape, values.dtype)],
        [ANY],
        [ANY],
        aliases={0: 0},
        cost=cost(micros),
    )(values)[0]


def cost(micros):
    return pl.CostEstimate(flops=micros * 1_150_000_000, bytes_accessed=0, transcendentals=0)


def shards(pic, cap, log_scale):
    width = pic.shape[1]
    long = width // LANE * OWN + PAD
    [img_out] = call(images_kernel, [shape((NXY, OWN, width), BF16)], [VM])(pic)
    img = hint(exchange(img_out), 10)
    [chip] = call(texts_kernel, [shape((NC, OWN, width), BF16)], [VM] * 2 + [ANY])(cap, swap(cap), img_out)
    own, other = gather(chip, 10)
    here = (NC + own.shape[0]) * OWN
    [part] = call(
        early_kernel,
        [shape((here, TILE), F32)],
        [SM] + [VM] * 3,
        scratch=[pltpu.VMEM((here, width), BF16)],
        cost=cost(3),
    )(log_scale, img, chip, own)
    rowp, colp = call(
        logits_kernel,
        [shape((NXY, 2 * NB, LANE), F32), shape((4 * NB, LANE), F32)],
        [SM, VM, VM, VM],
        scratch=[pltpu.VMEM((TILE, TILE), F32)],
    )(log_scale, img, part, other)
    rows = exchange(rowp)
    near = jnp.stack([colp, swap(colp)])
    columns = gather(near, 10)
    logits, txt = call(
        again_kernel,
        [shape((TILE, TILE), F32), shape((TILE, width), BF16)],
        [SM] + [VM] * 4 + [ANY],
        cost=cost(30),
    )(log_scale, img, chip, own, other, rows)
    half = (NZ, long, LANE)
    grad, keep, send, scalars = call(
        grad_kernel,
        [
            shape((TILE, TILE), BF16),
            shape(half, BF16),
            shape(half, BF16),
            shape((PAD, LANE), BF16),
        ],
        [SM] + [VM] * 6,
        scratch=[
            pltpu.VMEM((TILE, TILE), BF16),
            pltpu.VMEM((TILE, TILE), BF16),
            pltpu.VMEM((NC * NZ, 4 * NB, LANE), F32),
        ],
    )(log_scale, logits, img, rows, near, *columns)
    [terms] = call(
        terms_kernel,
        [shape((NXY, long, LANE), BF16)],
        [SM] + [VM] * 3,
        [ANY],
        scratch=[pltpu.VMEM((NXY, long, LANE), BF16), pltpu.SemaphoreType.DMA((width // (2 * LANE),))],
        cost=cost(4),
    )(log_scale, grad, txt, scalars)
    one, two, keep, far, terms = call(
        add_kernel,
        [
            shape((NC, long, LANE), BF16),
            shape((2 * NC, long, LANE), BF16),
            shape((long, LANE), BF16),
            shape((long, LANE), BF16),
            shape((NXY, long, LANE), BF16),
        ],
        [VM, VM, ANY],
        [VM] * 4 + [ANY],
        aliases={2: 4},
    )(keep, swap(send), terms)
    terms = exchange(terms)
    two = shift(two, 2)
    far = hint(shift(far, FAR), 5)
    [one] = call(relay_kernel, [shape((NC, long, LANE), BF16)], [VM] * 2, cost=cost(10))(one, two)
    one = shift(one, 1)
    [passed] = call(pass_kernel, [shape((long, LANE), BF16)], [VM] * 3, cost=cost(1))(one, two, far)
    return call(
        final_kernel,
        [shape((OWN, width), BF16), shape((OWN, width), BF16), shape((1,), F32), shape((1,), F32)],
        [VM] * 8,
        [VM, VM, SM, SM],
    )(pic, cap, terms, one, two, keep, far, swap(passed))


def solution(mesh):
    grid = Mesh(mesh.devices.reshape(NX, NC, NZ, NY), ("x", "c", "z", "y"))
    rows = P(("x", "c", "z", "y"), None)
    columns = P(("z", "y", "x", "c"), None)
    return jax.shard_map(
        shards,
        mesh=grid,
        in_specs=(rows, columns, P()),
        out_specs=(rows, columns, P(), P()),
        check_vma=False,
    )
```
